32 devices in a mesh: groups: 2 (over y), expert: 8 (over z, x), dp: 2 (over core).
Axes of the slice: x: 2, y: 2, z: 4, core: 2. Of those that a mesh axis runs over, the one named last changes fastest.
Arguments:
- normed: bfloat16 [672, 2048], P(('groups', 'expert'), 'dp'), parts along dimension 0, may hold values from -6 to 6
- cotangent: bfloat16 [672, 2048], P(('groups', 'expert'), 'dp'), parts along dimension 0, may hold values from -6 to 6
- expert_ids: int32 [672, 10], P(('groups', 'expert')), parts along dimension 0, may hold values from 0 to 23, all different within a row; in each aligned block of 42 rows (0 to 41, 42 to 83, ...) at most 28 rows name the same one
- route_weights: float32 [672, 10], P(('groups', 'expert')), parts along dimension 0, may hold values from 0.02 to 0.6
- w_gate: bfloat16 [24, 2048, 512], P('expert', 'dp'), may hold values from -0.125 to 0.125
- w_up: bfloat16 [24, 2048, 512], P('expert', 'dp'), may hold values from -0.125 to 0.125
- w_down: bfloat16 [24, 512, 2048], P('expert', None, 'dp'), may hold values from -0.25 to 0.25
Outputs:
- moe_out: bfloat16 [672, 2048], P(('groups', 'expert'), 'dp'), parts along dimension 0
- grad_normed: bfloat16 [672, 2048], P(('groups', 'expert'), 'dp'), parts along dimension 0
- grad_gate: bfloat16 [48, 2048, 512], P(('groups', 'expert'), 'dp'), parts along dimension 0
- grad_up: bfloat16 [48, 2048, 512], P(('groups', 'expert'), 'dp'), parts along dimension 0
- grad_down: bfloat16 [48, 512, 2048], P(('groups', 'expert'), None, 'dp'), parts along dimension 0
The draws below stay inside these ranges and needn't reach their ends.
There are 2 independent parts, one for each index of `groups`. The reference program is written for one: setup_inputs(seed, part) draws one part's arguments, and reference() takes and returns one part's arrays. A program takes and returns all parts, laid end to end along the dimension named above; an argument that names none is the same for every part. Nothing has to cross between parts.
Inputs may be any that keep to these rules, and one draw needn't show every extreme that they name: `expert_ids`: each row names 10 different experts. Among the rows of one index of expert (aligned blocks of 42 rows) no expert is named by more than 28 rows, and in every draw some expert is named by exactly 28 rows of some block.
All inputs are finite; a program needn't handle non-finite values.
Results may differ from the reference program's by a relative error of at most 0.0064.
Values may be sent and summed in bfloat16 or wider, within the bound.
A program may use at most 128 MiB of HBM per device.

```python
import math
import jax
import jax.numpy as jnp
import numpy as np
from jax import lax

D = 2048
F = 512
TOPK = 10
TOK_DEV = 42
EXPERTS = 24
TOKENS = 336
SCAP = 28
N_EXPERT = 8


def block_scale(key, dims, split, least, top_value):
    factor_of = 1.0
    for dim, blocks in split:
        steps = jax.random.uniform(jax.random.fold_in(jax.random.fold_in(key, 6), dim), (blocks,), jnp.float32, least / len(split), top_value / len(split))
        factor_of = factor_of * jnp.repeat(jnp.exp(steps), dims[dim] // blocks).reshape((-1,) + (1,) * (len(dims) - 1 - dim))
    return factor_of


def routed_block(stream_key, own, number, rows, count, top, most, slope):
    order = jax.random.permutation(stream_key, count)
    heavy_load, common = portions_of(count, rows * top, most, slope, True), portions_of(count, rows * top, most, slope, False)
    places = jnp.arange(count)

    def named(lengths, turn):
        used = int((lengths > 0).sum())
        fixed = max(1, used // 4)
        passed = fixed + (places - fixed + turn * (used - fixed)) % max(1, count - fixed)
        return jnp.zeros((count,), jnp.int32).at[order[jnp.where(places < fixed, places, passed)]].set(jnp.asarray(lengths, jnp.int32))

    lengths = jnp.where(number % 4 == 0, named(heavy_load, number // 4), named(common, number - number // 4 - 1))
    mixed = jax.random.permutation(jax.random.fold_in(own, 3), count)
    giver, receiver = mixed[0:count // 2 * 2:2], mixed[1:count // 2 * 2:2]
    margin = jnp.minimum(lengths[giver] - 1, most - lengths[receiver]) // 2
    margin = jnp.where((giver == order[0]) | (receiver == order[0]) | (lengths[receiver] == 0), 0, jnp.maximum(margin, 0))
    passed = jax.random.randint(jax.random.fold_in(own, 4), (count // 2,), 0, 1 << 20) % (margin + 1)
    lengths = lengths.at[giver].add(-passed).at[receiver].add(passed)
    labels = jnp.searchsorted(jnp.cumsum(lengths), jnp.arange(rows * top), side="right").astype(jnp.int32)
    grid = labels.reshape(top, rows).T
    grid = grid[jax.random.permutation(jax.random.fold_in(own, 1), rows)]
    turn = jax.random.randint(jax.random.fold_in(own, 2), (rows, 1), 0, top)
    return jnp.take_along_axis(grid, (jnp.arange(top)[None, :] + turn) % top, axis=1)


def portions_of(amount, total, limit, skew, full):
    loads = [(1 << 20) // math.isqrt(standing ** skew) + 1 for standing in range(1, amount + 1)]
    largest = limit if full else min(limit, max(-(-total // amount), total * loads[0] // sum(loads)))
    least = 1 if total - largest >= amount - 1 else 0
    counts, surplus = [largest] + [least] * (amount - 1), total - largest - least * (amount - 1)
    while surplus > 0:
        free = [i for i in range(1, amount) if counts[i] < largest] or [i for i in range(1, amount) if counts[i] < limit]
        whole, remaining = sum([loads[i] for i in free]), surplus
        for i in free:
            addition = min(limit - counts[i], max(1, remaining * loads[i] // whole), surplus)
            counts[i] = counts[i] + addition
            surplus = surplus - addition
    return np.array(counts)


def noise(own_key, dims, spread, limit, shards=(), kind=jnp.bfloat16):
    drawn = spread * jax.random.normal(own_key, dims, jnp.float32)
    if shards:
        drawn = drawn * block_scale(own_key, dims, shards, -0.22, 0.18)
    return jnp.clip(drawn, -limit, limit).astype(kind)


def setup_inputs(seed: int = 0, part: int = 0) -> dict:
    key_of = jax.random.split(jax.random.key(seed), 8)
    part_keys = jax.random.split(jax.random.fold_in(key_of[7], part), 8)
    normed = noise(part_keys[0], (TOKENS, D), 1.0, 6.0, ((0, 8), (1, 2)))
    cotangent = noise(part_keys[1], (TOKENS, D), 1.0, 6.0, ((0, 8), (1, 2)))
    expert_ids_keys = jax.random.split(jax.random.fold_in(part_keys[2], 1), TOKENS // TOK_DEV)
    expert_ids_turns = jax.random.permutation(jax.random.fold_in(part_keys[2], 3), TOKENS // TOK_DEV)
    expert_ids = jax.vmap(lambda own, number: routed_block(jax.random.fold_in(part_keys[2], 2), own, number, TOK_DEV, EXPERTS, TOPK, SCAP, 2))(expert_ids_keys, expert_ids_turns).reshape((TOKENS, TOPK))
    route_weights = jnp.clip(jnp.exp(math.log(0.6) - 3.4011974 * jax.random.uniform(part_keys[3], (TOKENS, TOPK), jnp.float32) ** block_scale(part_keys[3], (TOKENS, TOPK), ((0, 8),), -0.2, 0.2)), 0.02, 0.6)
    w_gate = noise(key_of[4], (EXPERTS, D, F), D ** -0.5, 0.125, ((0, 8), (1, 2)))
    w_up = noise(key_of[5], (EXPERTS, D, F), D ** -0.5, 0.125, ((0, 8), (1, 2)))
    w_down = noise(key_of[6], (EXPERTS, F, D), F ** -0.5, 0.25, ((0, 8), (2, 2)))
    return {"normed": normed, "cotangent": cotangent, "expert_ids": expert_ids, "route_weights": route_weights, "w_gate": w_gate, "w_up": w_up, "w_down": w_down}


def reference(normed, cotangent, expert_ids, route_weights, w_gate, w_up, w_down):
    assigned = TOKENS * TOPK
    per_expert = N_EXPERT * SCAP
    blocked = expert_ids.reshape(N_EXPERT, TOK_DEV * TOPK)
    onehot = (blocked[:, :, None] == jnp.arange(EXPERTS, dtype=jnp.int32)[None, None, :]).astype(jnp.int32)
    ranks = jnp.sum(onehot * jnp.cumsum(onehot, axis=1), axis=2) - 1
    source = jnp.arange(N_EXPERT, dtype=jnp.int32)[:, None]
    position = (blocked * per_expert + source * SCAP + ranks).reshape(-1).astype(jnp.int32)
    table = jnp.full((EXPERTS * per_expert,), assigned, jnp.int32)
    table = table.at[position].set(jnp.arange(assigned, dtype=jnp.int32)).reshape(EXPERTS, per_expert)
    scaled = (route_weights[:, :, None] * cotangent[:, None, :].astype(jnp.float32)).astype(jnp.bfloat16)
    scaled = scaled.reshape(assigned, D)
    x_padded = jnp.concatenate([normed, jnp.zeros((1, D), jnp.bfloat16)], axis=0)
    g_padded = jnp.concatenate([scaled, jnp.zeros((1, D), jnp.bfloat16)], axis=0)

    def one_expert(operands):
        index, gate_w, up_w, down_w = operands
        valid = index < assigned
        token = jnp.where(valid, index // TOPK, TOKENS).astype(jnp.int32)
        rows = x_padded[token]
        grads = g_padded[index]
        pre_gate = jnp.dot(rows, gate_w, preferred_element_type=jnp.float32)
        pre_up = jnp.dot(rows, up_w, preferred_element_type=jnp.float32)
        sig = jax.nn.sigmoid(pre_gate)
        hidden = (pre_gate * sig * pre_up).astype(jnp.bfloat16)
        out_rows = jnp.dot(hidden, down_w, preferred_element_type=jnp.float32).astype(jnp.bfloat16)
        hidden_grad = jnp.dot(grads, down_w.T, preferred_element_type=jnp.float32)
        gate_grad = (hidden_grad * pre_up * sig * (1.0 + pre_gate * (1.0 - sig))).astype(jnp.bfloat16)
        up_grad = (hidden_grad * pre_gate * sig).astype(jnp.bfloat16)
        row_grad = (jnp.dot(gate_grad, gate_w.T, preferred_element_type=jnp.float32)
                    + jnp.dot(up_grad, up_w.T, preferred_element_type=jnp.float32)).astype(jnp.bfloat16)
        grad_g = jnp.dot(rows.T, gate_grad, preferred_element_type=jnp.float32).astype(jnp.bfloat16)
        grad_u = jnp.dot(rows.T, up_grad, preferred_element_type=jnp.float32).astype(jnp.bfloat16)
        grad_d = jnp.dot(hidden.T, grads, preferred_element_type=jnp.float32).astype(jnp.bfloat16)
        return out_rows, row_grad, grad_g, grad_u, grad_d

    out_rows, row_grads, grad_gate, grad_up, grad_down = lax.map(one_expert, (table, w_gate, w_up, w_down))
    flat = table.reshape(-1)
    expert_out = jnp.zeros((assigned + 1, D), jnp.bfloat16).at[flat].set(out_rows.reshape(-1, D))[:assigned]
    row_grad = jnp.zeros((assigned + 1, D), jnp.bfloat16).at[flat].set(row_grads.reshape(-1, D))[:assigned]
    moe_out = jnp.sum(route_weights[:, :, None] * expert_out.reshape(TOKENS, TOPK, D).astype(jnp.float32), axis=1)
    grad_normed = jnp.sum(row_grad.reshape(TOKENS, TOPK, D).astype(jnp.float32), axis=1)
    return moe_out.astype(jnp.bfloat16), grad_normed.astype(jnp.bfloat16), grad_gate, grad_up, grad_down
```

```python
import functools

import jax
import jax.numpy as jnp
from jax import lax
from jax.experimental import pallas as pl
from jax.experimental.pallas import tpu as pltpu
from jax.sharding import PartitionSpec as P

F32, BF16 = jnp.float32, jnp.bfloat16
NN = (((1,), (0,)), ((), ()))
NT = (((1,), (1,)), ((), ()))
TN = (((0,), (0,)), ((), ()))
MESH = pl.DeviceIdType.MESH


def dot(a, b, dims):
    return lax.dot_general(a, b, dims, preferred_element_type=F32)


def kernel(n, rows, width, experts, x_in, c_in, wg_hbm, wu_hbm, wd_hbm,
           moe_ref, gn_ref, gg_hbm, gu_hbm, gd_hbm,
           xs, cs, xt, wg, wu, wd, own, snd, rcv, hid, gat, upg, part, red_out, red_in,
           out_g, out_u, out_d,
           w_sem, g_send, g_recv, d_send, d_recv, r_send, r_recv, o_sem):
    half = n // 2
    local = wg.shape[0]
    me_g, me_e, me_d = lax.axis_index("groups"), lax.axis_index("expert"), lax.axis_index("dp")
    z, col = me_e // 2, me_e % 2
    pos = z + col * (n - 1 - 2 * z)

    def at(place):
        place = (place + n) % n
        upper = place // half
        return 2 * place + upper * (2 * n - 1 - 4 * place)

    right = (me_g, at(pos + 1), me_d)
    left = (me_g, at(pos - 1), me_d)
    mate = (me_g, me_e, 1 - me_d)

    loads = [
        pltpu.make_async_copy(src, dst, w_sem.at[i])
        for i, (src, dst) in enumerate(((wg_hbm, wg), (wu_hbm, wu), (wd_hbm, wd)))
    ]
    for load in loads:
        load.start()

    barrier = pltpu.get_barrier_semaphore()
    for other in (left, right, mate):
        pl.semaphore_signal(barrier, inc=1, device_id=other, device_id_type=MESH)
    xs[pl.ds(0, rows), :] = x_in[...]
    cs[pl.ds(0, rows), :] = c_in[...]
    pl.semaphore_wait(barrier, 3)

    def slot(way, t):
        if t == 0:
            return 0
        if t == half:
            return n - 1
        return 2 * t - 1 + way

    def gather(way, arr, t):
        buf = (xs, cs)[arr]
        return pltpu.make_async_remote_copy(
            src_ref=buf.at[pl.ds(slot(way, t - 1) * rows, rows)],
            dst_ref=buf.at[pl.ds(slot(way, t) * rows, rows)],
            send_sem=g_send.at[way, arr, t - 1],
            recv_sem=g_recv.at[way, arr, t - 1],
            device_id=(right, left)[way],
            device_id_type=MESH,
        )

    def moves(t):
        if t < half:
            return [gather(0, 0, t), gather(1, 0, t), gather(0, 1, t), gather(1, 1, t)]
        return [gather(0, 0, t), gather(1, 1, t)]

    started = []

    def advance(t):
        later = {0: moves(t + 1)} if t < half else {0: []}
        if t == 0:
            for move in later[0]:
                move.start()
        elif t < half - 1:
            for now, move in zip(moves(t), later[0]):
                now.wait_recv()
                move.start()
        elif t == half - 1:
            now = moves(t)
            now[0].wait_recv()
            later[0][0].start()
            now[3].wait_recv()
            later[0][1].start()
            now[1].wait_recv()
            now[2].wait_recv()
        else:
            for now in moves(t):
                now.wait_recv()
        started.extend(later[0])

    early = (n // 4) * 2 + 1
    spans = ((0, early * rows), (early * rows, (n - early) * rows))

    def swap(chunk, j):
        span = pl.ds(*spans[chunk])
        return pltpu.make_async_remote_copy(
            src_ref=snd.at[j, :, span],
            dst_ref=rcv.at[j, :, span],
            send_sem=d_send.at[chunk, j],
            recv_sem=d_recv.at[chunk, j],
            device_id=mate,
            device_id_type=MESH,
        )

    def project(chunk):
        span = pl.ds(*spans[chunk])

        def body(j, carry):
            for m, value in enumerate((
                lambda: dot(xs[span, :], wg[j], NN),
                lambda: dot(xs[span, :], wu[j], NN),
                lambda: dot(cs[span, pl.ds(0, width)], wd[j], NT),
            )):
                result = value()
                own[j, m, span] = result
                snd[j, m, span] = result.astype(BF16)
            swap(chunk, j).start()
            return carry

        lax.fori_loop(0, local, body, 0)

    def activate(chunk):
        first, count = spans[chunk]
        span = pl.ds(first, count)

        def body(j, carry):
            swap(chunk, j).wait_recv()
            tail = cs[span, pl.ds(width, cs.shape[1] - width)].astype(F32)
            lane = lax.broadcasted_iota(jnp.int32, tail.shape, 1)
            mine = me_e * local + j
            p = jnp.sum(
                jnp.where((lane == mine) | (lane == mine + experts), tail, 0.0), axis=1, keepdims=True
            )
            gate = own[j, 0, span] + rcv[j, 0, span].astype(F32)
            up = own[j, 1, span] + rcv[j, 1, span].astype(F32)
            back = p * (own[j, 2, span] + rcv[j, 2, span].astype(F32))
            sig = jax.nn.sigmoid(gate)
            act = gate * sig
            hid[j, span] = (p * (act * up)).astype(BF16)
            gat[j, span] = (back * up * sig * (1.0 + gate * (1.0 - sig))).astype(BF16)
            upg[j, span] = (back * act).astype(BF16)
            return carry

        lax.fori_loop(0, local, body, 0)

    def combine(chunk):
        span = pl.ds(*spans[chunk])
        part[0, span] = dot(hid[0, span], wd[0], NN)
        part[1, span] = dot(gat[0, span], wg[0], NT) + dot(upg[0, span], wu[0], NT)

        def body(j, carry):
            part[0, span] += dot(hid[j, span], wd[j], NN)
            part[1, span] += dot(gat[j, span], wg[j], NT) + dot(upg[j, span], wu[j], NT)
            return carry

        lax.fori_loop(1, local, body, 0)

    for t in range(n // 4 + 1):
        advance(t)
    for load in loads:
        load.wait()
    project(0)
    for t in range(n // 4 + 1, half):
        advance(t)
    activate(0)
    combine(0)
    advance(half)
    project(1)
    xt[...] = xs[...].T
    activate(1)
    combine(1)

    def ring(way, arr, d):
        return pltpu.make_async_remote_copy(
            src_ref=red_out.at[way, arr, d - 1],
            dst_ref=red_in.at[way, arr, d - 1],
            send_sem=r_send.at[way, arr, d - 1],
            recv_sem=r_recv.at[way, arr, d - 1],
            device_id=(right, left)[way],
            device_id_type=MESH,
        )

    def forward(way, arr, d):
        value = part[arr, pl.ds(slot(1 - way, d) * rows, rows)]
        if d < half - 1 or (d == half - 1 and arr == way):
            ring(way, arr, d + 1).wait_recv()
            value = value + red_in[way, arr, d].astype(F32)
        red_out[way, arr, d - 1] = value.astype(BF16)
        move = ring(way, arr, d)
        move.start()
        started.append(move)

    writes = []

    def weight_grad(j, kind):
        buf, hbm = ((out_g, gg_hbm), (out_u, gu_hbm), (out_d, gd_hbm))[kind]
        if kind == 0:
            buf[j] = dot(xt[...], gat[j], NN).astype(BF16)
        elif kind == 1:
            buf[j] = dot(xt[...], upg[j], NN).astype(BF16)
        else:
            buf[j] = dot(hid[j], cs[:, pl.ds(0, width)], TN).astype(BF16)
        copy = pltpu.make_async_copy(buf.at[j], hbm.at[j], o_sem.at[kind, j])
        copy.start()
        writes.append(copy)

    jobs = [(j, kind) for j in range(local) for kind in range(3)]
    ticks = [(0, half)]
    for d in range(half - 1, 0, -1):
        ticks += [(1, d), (0, d)]
    for i, (arr, d) in enumerate(ticks):
        forward(0, arr, d)
        forward(1, 1 - arr, d)
        if i >= 1:
            take = -(-len(jobs) // (len(ticks) - i))
            for job in jobs[:take]:
                weight_grad(*job)
            jobs = jobs[take:]

    for arr, ref in ((0, moe_ref), (1, gn_ref)):
        total = part[arr, pl.ds(0, rows)]
        for way in range(2):
            ring(way, arr, 1).wait_recv()
            total = total + red_in[way, arr, 0].astype(F32)
        ref[...] = total.astype(BF16)

    for move in started:
        move.wait_send()
    for chunk in range(2):
        for j in range(local):
            swap(chunk, j).wait_send()
    for copy in writes:
        copy.wait()


def fused(normed, cotangent, routes, w_gate, w_up, w_down):
    tok_rows, width = normed.shape
    local, _, hidden = w_gate.shape
    n = lax.axis_size("expert")
    experts = routes.shape[1]
    rows = -(-tok_rows // 16) * 16
    pad = rows - tok_rows
    tail = -(-2 * experts // 128) * 128
    high = lax.reduce_precision(routes, 8, 7)
    coded = jnp.concatenate([high, routes - high], axis=1).astype(BF16)
    coded = jnp.pad(coded, ((0, pad), (0, tail - 2 * experts)))
    x_in = jnp.pad(normed, ((0, pad), (0, 0)))
    c_in = jnp.concatenate([jnp.pad(cotangent, ((0, pad), (0, 0))), coded], axis=1)
    total, half = n * rows, n // 2
    any_spec, vmem_spec = pl.BlockSpec(memory_space=pl.ANY), pl.BlockSpec(memory_space=pltpu.VMEM)
    dma = pltpu.SemaphoreType.DMA
    moe, grad, gg, gu, gd = pl.pallas_call(
        functools.partial(kernel, n, rows, width, experts),
        out_shape=(
            jax.ShapeDtypeStruct((rows, width), BF16),
            jax.ShapeDtypeStruct((rows, width), BF16),
            jax.ShapeDtypeStruct(w_gate.shape, BF16),
            jax.ShapeDtypeStruct(w_up.shape, BF16),
            jax.ShapeDtypeStruct(w_down.shape, BF16),
        ),
        in_specs=[vmem_spec, vmem_spec, any_spec, any_spec, any_spec],
        out_specs=(vmem_spec, vmem_spec, any_spec, any_spec, any_spec),
        scratch_shapes=[
            pltpu.VMEM((total, width), BF16),
            pltpu.VMEM((total, width + tail), BF16),
            pltpu.VMEM((width, total), BF16),
            pltpu.VMEM(w_gate.shape, BF16),
            pltpu.VMEM(w_up.shape, BF16),
            pltpu.VMEM(w_down.shape, BF16),
            pltpu.VMEM((local, 3, total, hidden), F32),
            pltpu.VMEM((local, 3, total, hidden), BF16),
            pltpu.VMEM((local, 3, total, hidden), BF16),
            pltpu.VMEM((local, total, hidden), BF16),
            pltpu.VMEM((local, total, hidden), BF16),
            pltpu.VMEM((local, total, hidden), BF16),
            pltpu.VMEM((2, total, width), F32),
            pltpu.VMEM((2, 2, half, rows, width), BF16),
            pltpu.VMEM((2, 2, half, rows, width), BF16),
            pltpu.VMEM(w_gate.shape, BF16),
            pltpu.VMEM(w_up.shape, BF16),
            pltpu.VMEM(w_down.shape, BF16),
            dma((3,)),
            dma((2, 2, half)),
            dma((2, 2, half)),
            dma((2, local)),
            dma((2, local)),
            dma((2, 2, half)),
            dma((2, 2, half)),
            dma((3, local)),
        ],
        compiler_params=pltpu.CompilerParams(
            collective_id=0, has_side_effects=True, vmem_limit_bytes=60 * 2**20
        ),
    )(x_in, c_in, w_gate, w_up, w_down)
    return moe[:tok_rows], grad[:tok_rows], gg, gu, gd


def plain(normed, cotangent, routes, w_gate, w_up, w_down):
    local = w_gate.shape[0]
    rows = lax.all_gather(normed, "expert", axis=0, tiled=True)
    grads = lax.all_gather(cotangent, "expert", axis=0, tiled=True)
    probs = lax.all_gather(routes, "expert", axis=0, tiled=True)
    probs = lax.dynamic_slice_in_dim(probs, lax.axis_index("expert") * local, local, axis=1)
    p = probs.T[:, :, None]
    ein = functools.partial(jnp.einsum, preferred_element_type=F32)
    gate, up, back = lax.psum(
        (ein("rd,jdf->jrf", rows, w_gate), ein("rd,jdf->jrf", rows, w_up), ein("rd,jfd->jrf", grads, w_down)),
        "dp",
    )
    back = p * back
    sig = jax.nn.sigmoid(gate)
    act = gate * sig
    hid = (p * (act * up)).astype(BF16)
    gat = (back * up * sig * (1.0 + gate * (1.0 - sig))).astype(BF16)
    upg = (back * act).astype(BF16)
    moe = ein("jrf,jfd->rd", hid, w_down)
    grad = ein("jrf,jdf->rd", gat, w_gate) + ein("jrf,jdf->rd", upg, w_up)
    return (
        lax.psum_scatter(moe, "expert", scatter_dimension=0, tiled=True).astype(BF16),
        lax.psum_scatter(grad, "expert", scatter_dimension=0, tiled=True).astype(BF16),
        ein("rd,jrf->jdf", rows, gat).astype(BF16),
        ein("rd,jrf->jdf", rows, upg).astype(BF16),
        ein("jrf,rd->jfd", hid, grads).astype(BF16),
    )


def shards(normed, cotangent, expert_ids, route_weights, w_gate, w_up, w_down):
    n, pair = lax.axis_size("expert"), lax.axis_size("dp")
    experts = w_gate.shape[0] * n
    chosen = expert_ids[:, :, None] == jnp.arange(experts, dtype=jnp.int32)[None, None, :]
    routes = jnp.sum(jnp.where(chosen, route_weights[:, :, None], 0.0), axis=1)
    form = fused if pair == 2 and 4 <= n <= 8 and n % 4 == 0 else plain
    return form(normed, cotangent, routes, w_gate, w_up, w_down)


def solution(mesh):
    in_specs = (
        P(("groups", "expert"), "dp"),
        P(("groups", "expert"), "dp"),
        P(("groups", "expert"), None),
        P(("groups", "expert"), None),
        P("expert", "dp", None),
        P("expert", "dp", None),
        P("expert", None, "dp"),
    )
    out_specs = (
        P(("groups", "expert"), "dp"),
        P(("groups", "expert"), "dp"),
        P(("groups", "expert"), "dp", None),
        P(("groups", "expert"), "dp", None),
        P(("groups", "expert"), None, "dp"),
    )
    return jax.shard_map(shards, mesh=mesh, in_specs=in_specs, out_specs=out_specs, check_vma=False)
```

```python
import functools

import jax
import jax.numpy as jnp
from jax import lax
from jax.experimental import pallas as pl
from jax.experimental.pallas import tpu as pltpu
from jax.sharding import PartitionSpec as P

F32, BF16 = jnp.float32, jnp.bfloat16
NN = (((1,), (0,)), ((), ()))
NT = (((1,), (1,)), ((), ()))
TN = (((0,), (0,)), ((), ()))
MESH = pl.DeviceIdType.MESH


def dot(a, b, dims):
    return lax.dot_general(a, b, dims, preferred_element_type=F32)


def kernel(n, rows, width, experts, x_in, c_in, ids, weights, wg_hbm, wu_hbm, wd_hbm,
           moe_ref, gn_ref, gg_ref, gu_ref, gd_ref,
           xs, cs, xt, wg, wu, wd, own, snd, rcv, hid, gat, upg, part, red_out, red_in,
           w_sem, g_send, g_recv, d_send, d_recv, r_send, r_recv):
    half = n // 2
    local = wg.shape[0]
    me_g, me_e, me_d = lax.axis_index("groups"), lax.axis_index("expert"), lax.axis_index("dp")
    z, col = me_e // 2, me_e % 2
    pos = z + col * (n - 1 - 2 * z)

    def at(place):
        place = (place + n) % n
        upper = place // half
        return 2 * place + upper * (2 * n - 1 - 4 * place)

    right = (me_g, at(pos + 1), me_d)
    left = (me_g, at(pos - 1), me_d)
    mate = (me_g, me_e, 1 - me_d)

    loads = [
        pltpu.make_async_copy(src, dst, w_sem.at[i])
        for i, (src, dst) in enumerate(((wg_hbm, wg), (wu_hbm, wu), (wd_hbm, wd)))
    ]
    for load in loads:
        load.start()

    barrier = pltpu.get_barrier_semaphore()
    for other in (left, right, mate):
        pl.semaphore_signal(barrier, inc=1, device_id=other, device_id_type=MESH)
    tokens = x_in.shape[0]
    if rows > tokens:
        part[:, pl.ds(tokens, rows - tokens), :] = jnp.zeros((2, rows - tokens, width), F32)
    part[0, pl.ds(0, tokens), :] = x_in[...].astype(F32)
    part[1, pl.ds(0, tokens), :] = c_in[...].astype(F32)
    xs[pl.ds(0, rows), :] = part[0, pl.ds(0, rows), :].astype(BF16)
    cs[pl.ds(0, rows), pl.ds(0, width)] = part[1, pl.ds(0, rows), :].astype(BF16)
    tail = cs.shape[1] - width
    place = lax.broadcasted_iota(jnp.int32, (tail, tokens), 0)
    high, low = jnp.zeros((tail, tokens), F32), jnp.zeros((tail, tokens), F32)
    for k in range(ids.shape[0]):
        name, weight = ids[pl.ds(k, 1), :], weights[pl.ds(k, 1), :]
        high = high + jnp.where(place == name, weight, 0.0)
        low = low + jnp.where(place == name + experts, weight, 0.0)
    low = low - low.astype(BF16).astype(F32)
    part[0, pl.ds(0, tail), pl.ds(0, 128)] = jnp.zeros((tail, 128), F32)
    part[0, pl.ds(0, tail), pl.ds(0, tokens)] = high + low
    cs[pl.ds(0, rows), pl.ds(width, tail)] = part[0, pl.ds(0, tail), pl.ds(0, 128)].T[:rows].astype(BF16)
    pl.semaphore_wait(barrier, 3)

    def slot(way, t):
        if t == 0:
            return 0
        if t == half:
            return n - 1
        return 2 * t - 1 + way

    def gather(way, arr, t):
        buf = (xs, cs)[arr]
        return pltpu.make_async_remote_copy(
            src_ref=buf.at[pl.ds(slot(way, t - 1) * rows, rows)],
            dst_ref=buf.at[pl.ds(slot(way, t) * rows, rows)],
            send_sem=g_send.at[way, arr, t - 1],
            recv_sem=g_recv.at[way, arr, t - 1],
            device_id=(right, left)[way],
            device_id_type=MESH,
        )

    def moves(t):
        if t < half:
            return [gather(0, 0, t), gather(1, 0, t), gather(0, 1, t), gather(1, 1, t)]
        return [gather(0, 0, t), gather(1, 1, t)]

    started = []

    def advance(t):
        later = {0: moves(t + 1)} if t < half else {0: []}
        if t == 0:
            for move in later[0]:
                move.start()
        elif t < half - 1:
            for now, move in zip(moves(t), later[0]):
                now.wait_recv()
                move.start()
        elif t == half - 1:
            now = moves(t)
            now[0].wait_recv()
            later[0][0].start()
            now[3].wait_recv()
            later[0][1].start()
            now[1].wait_recv()
            now[2].wait_recv()
        else:
            for now in moves(t):
                now.wait_recv()
        started.extend(later[0])

    early = (n // 4) * 2 + 1
    spans = ((0, early * rows), (early * rows, (n - early) * rows))

    def swap(chunk, j):
        span = pl.ds(*spans[chunk])
        return pltpu.make_async_remote_copy(
            src_ref=snd.at[j, :, span],
            dst_ref=rcv.at[j, :, span],
            send_sem=d_send.at[chunk, j],
            recv_sem=d_recv.at[chunk, j],
            device_id=mate,
            device_id_type=MESH,
        )

    def project(chunk):
        span = pl.ds(*spans[chunk])

        def body(j, carry):
            for m, value in enumerate((
                lambda: dot(xs[span, :], wg[j], NN),
                lambda: dot(xs[span, :], wu[j], NN),
                lambda: dot(cs[span, pl.ds(0, width)], wd[j], NT),
            )):
                result = value()
                own[j, m, span] = result
                snd[j, m, span] = result.astype(BF16)
            swap(chunk, j).start()
            return carry

        lax.fori_loop(0, local, body, 0)

    def activate(chunk):
        first, count = spans[chunk]
        span = pl.ds(first, count)

        def body(j, carry):
            swap(chunk, j).wait_recv()
            tail = cs[span, pl.ds(width, cs.shape[1] - width)].astype(F32)
            lane = lax.broadcasted_iota(jnp.int32, tail.shape, 1)
            mine = me_e * local + j
            p = jnp.sum(
                jnp.where((lane == mine) | (lane == mine + experts), tail, 0.0), axis=1, keepdims=True
            )
            gate = own[j, 0, span] + rcv[j, 0, span].astype(F32)
            up = own[j, 1, span] + rcv[j, 1, span].astype(F32)
            back = p * (own[j, 2, span] + rcv[j, 2, span].astype(F32))
            sig = jax.nn.sigmoid(gate)
            act = gate * sig
            hid[j, span] = (p * (act * up)).astype(BF16)
            gat[j, span] = (back * up * sig * (1.0 + gate * (1.0 - sig))).astype(BF16)
            upg[j, span] = (back * act).astype(BF16)
            return carry

        lax.fori_loop(0, local, body, 0)

    def combine(chunk):
        span = pl.ds(*spans[chunk])
        part[0, span] = dot(hid[0, span], wd[0], NN)
        part[1, span] = dot(gat[0, span], wg[0], NT) + dot(upg[0, span], wu[0], NT)

        def body(j, carry):
            part[0, span] += dot(hid[j, span], wd[j], NN)
            part[1, span] += dot(gat[j, span], wg[j], NT) + dot(upg[j, span], wu[j], NT)
            return carry

        lax.fori_loop(1, local, body, 0)

    for t in range(n // 4 + 1):
        advance(t)
    for load in loads:
        load.wait()
    project(0)
    for t in range(n // 4 + 1, half):
        advance(t)
    activate(0)
    combine(0)
    advance(half)
    project(1)
    xt[...] = xs[...].T
    activate(1)
    combine(1)

    def ring(way, arr, d):
        return pltpu.make_async_remote_copy(
            src_ref=red_out.at[way, arr, d - 1],
            dst_ref=red_in.at[way, arr, d - 1],
            send_sem=r_send.at[way, arr, d - 1],
            recv_sem=r_recv.at[way, arr, d - 1],
            device_id=(right, left)[way],
            device_id_type=MESH,
        )

    def forward(way, arr, d):
        value = part[arr, pl.ds(slot(1 - way, d) * rows, rows)]
        if d < half - 1 or (d == half - 1 and arr == way):
            ring(way, arr, d + 1).wait_recv()
            value = value + red_in[way, arr, d].astype(F32)
        red_out[way, arr, d - 1] = value.astype(BF16)
        move = ring(way, arr, d)
        move.start()
        started.append(move)

    def weight_grad(j, kind):
        buf = (gg_ref, gu_ref, gd_ref)[kind]
        if kind == 0:
            buf[j] = dot(xt[...], gat[j], NN).astype(BF16)
        elif kind == 1:
            buf[j] = dot(xt[...], upg[j], NN).astype(BF16)
        else:
            buf[j] = dot(hid[j], cs[:, pl.ds(0, width)], TN).astype(BF16)

    jobs = [(j, kind) for j in range(local) for kind in range(3)]
    ticks = [(0, half)]
    for d in range(half - 1, 0, -1):
        ticks += [(1, d), (0, d)]
    for i, (arr, d) in enumerate(ticks):
        forward(0, arr, d)
        forward(1, 1 - arr, d)
        if i >= 1:
            take = -(-len(jobs) // (len(ticks) - i))
            for job in jobs[:take]:
                weight_grad(*job)
            jobs = jobs[take:]

    for arr, ref in ((0, moe_ref), (1, gn_ref)):
        total = part[arr, pl.ds(0, rows)]
        for way in range(2):
            ring(way, arr, 1).wait_recv()
            total = total + red_in[way, arr, 0].astype(F32)
        part[arr, pl.ds(0, rows)] = total
        ref[...] = part[arr, pl.ds(0, tokens)].astype(BF16)

    for move in started:
        move.wait_send()
    for chunk in range(2):
        for j in range(local):
            swap(chunk, j).wait_send()


def deliver(moe, grad, gg, gu, gd, moe_out, grad_out, gg_out, gu_out, gd_out, sem):
    copies = [
        pltpu.make_async_copy(src.at[j], dst.at[j], sem.at[i, j])
        for i, (src, dst) in enumerate(((gg, gg_out), (gu, gu_out), (gd, gd_out)))
        for j in range(src.shape[0])
    ]
    for copy in copies:
        copy.start()
    moe_out[...] = moe[...]
    grad_out[...] = grad[...]
    for copy in copies:
        copy.wait()


def fused(normed, cotangent, expert_ids, route_weights, w_gate, w_up, w_down):
    tok_rows, width = normed.shape
    local, _, hidden = w_gate.shape
    n = lax.axis_size("expert")
    experts = local * n
    rows = -(-tok_rows // 16) * 16
    tail = -(-2 * experts // 128) * 128
    total, half = n * rows, n // 2
    any_spec, vmem_spec = pl.BlockSpec(memory_space=pl.ANY), pl.BlockSpec(memory_space=pltpu.VMEM)
    dma = pltpu.SemaphoreType.DMA
    moe, grad, gg, gu, gd = pl.pallas_call(
        functools.partial(kernel, n, rows, width, experts),
        out_shape=(
            pltpu.VMEM((tok_rows, width), BF16),
            pltpu.VMEM((tok_rows, width), BF16),
            pltpu.VMEM(w_gate.shape, BF16),
            pltpu.VMEM(w_up.shape, BF16),
            pltpu.VMEM(w_down.shape, BF16),
        ),
        in_specs=[vmem_spec, vmem_spec, vmem_spec, vmem_spec, any_spec, any_spec, any_spec],
        out_specs=(vmem_spec, vmem_spec, vmem_spec, vmem_spec, vmem_spec),
        scratch_shapes=[
            pltpu.VMEM((total, width), BF16),
            pltpu.VMEM((total, width + tail), BF16),
            pltpu.VMEM((width, total), BF16),
            pltpu.VMEM(w_gate.shape, BF16),
            pltpu.VMEM(w_up.shape, BF16),
            pltpu.VMEM(w_down.shape, BF16),
            pltpu.VMEM((local, 3, total, hidden), F32),
            pltpu.VMEM((local, 3, total, hidden), BF16),
            pltpu.VMEM((local, 3, total, hidden), BF16),
            pltpu.VMEM((local, total, hidden), BF16),
            pltpu.VMEM((local, total, hidden), BF16),
            pltpu.VMEM((local, total, hidden), BF16),
            pltpu.VMEM((2, total, width), F32),
            pltpu.VMEM((2, 2, half, rows, width), BF16),
            pltpu.VMEM((2, 2, half, rows, width), BF16),
            dma((3,)),
            dma((2, 2, half)),
            dma((2, 2, half)),
            dma((2, local)),
            dma((2, local)),
            dma((2, 2, half)),
            dma((2, 2, half)),
        ],
        compiler_params=pltpu.CompilerParams(
            collective_id=0, has_side_effects=True, vmem_limit_bytes=46 * 2**20
        ),
    )(normed, cotangent, expert_ids.T, route_weights.T, w_gate, w_up, w_down)
    moe, grad, gg, gu, gd = (pltpu.with_memory_space_constraint(a, pltpu.VMEM) for a in (moe, grad, gg, gu, gd))
    shapes = tuple(jax.ShapeDtypeStruct(a.shape, BF16) for a in (moe, grad, gg, gu, gd))
    return pl.pallas_call(
        deliver,
        out_shape=shapes,
        in_specs=[vmem_spec] * 5,
        out_specs=(vmem_spec, vmem_spec, any_spec, any_spec, any_spec),
        scratch_shapes=[dma((3, local))],
        compiler_params=pltpu.CompilerParams(vmem_limit_bytes=4 * 2**20),
    )(moe, grad, gg, gu, gd)


def plain(normed, cotangent, routes, w_gate, w_up, w_down):
    local = w_gate.shape[0]
    rows = lax.all_gather(normed, "expert", axis=0, tiled=True)
    grads = lax.all_gather(cotangent, "expert", axis=0, tiled=True)
    probs = lax.all_gather(routes, "expert", axis=0, tiled=True)
    probs = lax.dynamic_slice_in_dim(probs, lax.axis_index("expert") * local, local, axis=1)
    p = probs.T[:, :, None]
    ein = functools.partial(jnp.einsum, preferred_element_type=F32)
    gate, up, back = lax.psum(
        (ein("rd,jdf->jrf", rows, w_gate), ein("rd,jdf->jrf", rows, w_up), ein("rd,jfd->jrf", grads, w_down)),
        "dp",
    )
    back = p * back
    sig = jax.nn.sigmoid(gate)
    act = gate * sig
    hid = (p * (act * up)).astype(BF16)
    gat = (back * up * sig * (1.0 + gate * (1.0 - sig))).astype(BF16)
    upg = (back * act).astype(BF16)
    moe = ein("jrf,jfd->rd", hid, w_down)
    grad = ein("jrf,jdf->rd", gat, w_gate) + ein("jrf,jdf->rd", upg, w_up)
    return (
        lax.psum_scatter(moe, "expert", scatter_dimension=0, tiled=True).astype(BF16),
        lax.psum_scatter(grad, "expert", scatter_dimension=0, tiled=True).astype(BF16),
        ein("rd,jrf->jdf", rows, gat).astype(BF16),
        ein("rd,jrf->jdf", rows, upg).astype(BF16),
        ein("jrf,rd->jfd", hid, grads).astype(BF16),
    )


def shards(normed, cotangent, expert_ids, route_weights, w_gate, w_up, w_down):
    n, pair = lax.axis_size("expert"), lax.axis_size("dp")
    experts = w_gate.shape[0] * n
    if pair == 2 and 4 <= n <= 8 and n % 4 == 0:
        return fused(normed, cotangent, expert_ids, route_weights, w_gate, w_up, w_down)
    chosen = expert_ids[:, :, None] == jnp.arange(experts, dtype=jnp.int32)[None, None, :]
    routes = jnp.sum(jnp.where(chosen, route_weights[:, :, None], 0.0), axis=1)
    return plain(normed, cotangent, routes, w_gate, w_up, w_down)


def solution(mesh):
    in_specs = (
        P(("groups", "expert"), "dp"),
        P(("groups", "expert"), "dp"),
        P(("groups", "expert"), None),
        P(("groups", "expert"), None),
        P("expert", "dp", None),
        P("expert", "dp", None),
        P("expert", None, "dp"),
    )
    out_specs = (
        P(("groups", "expert"), "dp"),
        P(("groups", "expert"), "dp"),
        P(("groups", "expert"), "dp", None),
        P(("groups", "expert"), "dp", None),
        P(("groups", "expert"), None, "dp"),
    )
    return jax.shard_map(shards, mesh=mesh, in_specs=in_specs, out_specs=out_specs, check_vma=False)
```

```python
import functools

import jax
import jax.numpy as jnp
from jax import lax
from jax.experimental import pallas as pl
from jax.experimental.pallas import tpu as pltpu
from jax.sharding import PartitionSpec as P

F32, BF16 = jnp.float32, jnp.bfloat16
NN = (((1,), (0,)), ((), ()))
NT = (((1,), (1,)), ((), ()))
TN = (((0,), (0,)), ((), ()))
MESH = pl.DeviceIdType.MESH


def dot(a, b, dims):
    return lax.dot_general(a, b, dims, preferred_element_type=F32)


def kernel(n, rows, width, experts, x_in, c_in, ids, weights, wg_hbm, wu_hbm, wd_hbm,
           moe_ref, gn_ref, gg_ref, gu_ref, gd_ref,
           xs, cs, xt, wg, wu, wd, own, snd, rcv, hid, gat, upg, part, red_out, red_in,
           w_sem, g_send, g_recv, d_send, d_recv, r_send, r_recv):
    half = n // 2
    local = wg.shape[0]
    cut = rows * 2 // 3 // 16 * 16
    sizes, offsets, bases = (cut, rows - cut), (0, cut), (0, n * cut)
    spans = ((0, n * cut), (n * cut, n * (rows - cut)))
    me_g, me_e, me_d = lax.axis_index("groups"), lax.axis_index("expert"), lax.axis_index("dp")
    z, col = me_e // 2, me_e % 2
    pos = z + col * (n - 1 - 2 * z)

    def at(place):
        place = (place + n) % n
        upper = place // half
        return 2 * place + upper * (2 * n - 1 - 4 * place)

    right = (me_g, at(pos + 1), me_d)
    left = (me_g, at(pos - 1), me_d)
    mate = (me_g, me_e, 1 - me_d)

    loads = [
        pltpu.make_async_copy(src, dst, w_sem.at[i])
        for i, (src, dst) in enumerate(((wg_hbm, wg), (wu_hbm, wu), (wd_hbm, wd)))
    ]
    for load in loads:
        load.start()

    barrier = pltpu.get_barrier_semaphore()
    for other in (left, right, mate):
        pl.semaphore_signal(barrier, inc=1, device_id=other, device_id_type=MESH)
    tokens = x_in.shape[0]
    if rows > tokens:
        part[:, pl.ds(tokens, rows - tokens), :] = jnp.zeros((2, rows - tokens, width), F32)
    part[0, pl.ds(0, tokens), :] = x_in[...].astype(F32)
    part[1, pl.ds(0, tokens), :] = c_in[...].astype(F32)
    for size, offset, base in zip(sizes, offsets, bases):
        xs[pl.ds(base, size), :] = part[0, pl.ds(offset, size), :].astype(BF16)
        cs[pl.ds(base, size), pl.ds(0, width)] = part[1, pl.ds(offset, size), :].astype(BF16)
    tail = cs.shape[1] - width
    place = lax.broadcasted_iota(jnp.int32, (tail, tokens), 0)
    high, low = jnp.zeros((tail, tokens), F32), jnp.zeros((tail, tokens), F32)
    for k in range(ids.shape[0]):
        name, weight = ids[pl.ds(k, 1), :], weights[pl.ds(k, 1), :]
        high = high + jnp.where(place == name, weight, 0.0)
        low = low + jnp.where(place == name + experts, weight, 0.0)
    low = low - low.astype(BF16).astype(F32)
    part[0, pl.ds(0, tail), pl.ds(0, 128)] = jnp.zeros((tail, 128), F32)
    part[0, pl.ds(0, tail), pl.ds(0, tokens)] = high + low
    coded = part[0, pl.ds(0, tail), pl.ds(0, 128)].T
    for size, offset, base in zip(sizes, offsets, bases):
        cs[pl.ds(base, size), pl.ds(width, tail)] = coded[offset:offset + size].astype(BF16)
    pl.semaphore_wait(barrier, 3)

    def slot(way, t):
        if t == 0:
            return 0
        if t == half:
            return n - 1
        return 2 * t - 1 + way

    def gather(phase, way, arr, t):
        base, size = bases[phase], sizes[phase]
        buf = (xs, cs)[arr]
        return pltpu.make_async_remote_copy(
            src_ref=buf.at[pl.ds(base + slot(way, t - 1) * size, size)],
            dst_ref=buf.at[pl.ds(base + slot(way, t) * size, size)],
            send_sem=g_send.at[phase, way, arr, t - 1],
            recv_sem=g_recv.at[phase, way, arr, t - 1],
            device_id=(right, left)[way],
            device_id_type=MESH,
        )

    def moves(phase, t):
        if t < half:
            return [gather(phase, way, arr, t) for arr in range(2) for way in range(2)]
        return [gather(phase, 0, 0, t), gather(phase, 1, 1, t)]

    started = []

    def advance(phase, t):
        now = moves(phase, t) if t > 0 else []
        later = moves(phase, t + 1) if t < half else []
        started.extend(later)
        if t == 0:
            for move in later:
                move.start()
        elif t < half - 1:
            for arrived, move in zip(now, later):
                arrived.wait_recv()
                move.start()
        elif t == half - 1:
            now[0].wait_recv()
            later[0].start()
            now[3].wait_recv()
            later[1].start()
            now[1].wait_recv()
            now[2].wait_recv()
        else:
            for arrived in now:
                arrived.wait_recv()

    def swap(chunk, j):
        span = pl.ds(*spans[chunk])
        return pltpu.make_async_remote_copy(
            src_ref=snd.at[j, :, span],
            dst_ref=rcv.at[j, :, span],
            send_sem=d_send.at[chunk, j],
            recv_sem=d_recv.at[chunk, j],
            device_id=mate,
            device_id_type=MESH,
        )

    def project(chunk):
        span = pl.ds(*spans[chunk])

        def body(j, carry):
            for m, value in enumerate((
                lambda: dot(xs[span, :], wg[j], NN),
                lambda: dot(xs[span, :], wu[j], NN),
                lambda: dot(cs[span, pl.ds(0, width)], wd[j], NT),
            )):
                result = value()
                own[j, m, span] = result
                snd[j, m, span] = result.astype(BF16)
            swap(chunk, j).start()
            return carry

        lax.fori_loop(0, local, body, 0)

    def activate(chunk):
        first, count = spans[chunk]
        span = pl.ds(first, count)

        def body(j, carry):
            swap(chunk, j).wait_recv()
            tail = cs[span, pl.ds(width, cs.shape[1] - width)].astype(F32)
            lane = lax.broadcasted_iota(jnp.int32, tail.shape, 1)
            mine = me_e * local + j
            p = jnp.sum(
                jnp.where((lane == mine) | (lane == mine + experts), tail, 0.0), axis=1, keepdims=True
            )
            gate = own[j, 0, span] + rcv[j, 0, span].astype(F32)
            up = own[j, 1, span] + rcv[j, 1, span].astype(F32)
            back = p * (own[j, 2, span] + rcv[j, 2, span].astype(F32))
            sig = jax.nn.sigmoid(gate)
            act = gate * sig
            hid[j, span] = (p * (act * up)).astype(BF16)
            gat[j, span] = (back * up * sig * (1.0 + gate * (1.0 - sig))).astype(BF16)
            upg[j, span] = (back * act).astype(BF16)
            return carry

        lax.fori_loop(0, local, body, 0)

    def combine(chunk):
        span = pl.ds(*spans[chunk])
        part[0, span] = dot(hid[0, span], wd[0], NN)
        part[1, span] = dot(gat[0, span], wg[0], NT) + dot(upg[0, span], wu[0], NT)

        def body(j, carry):
            part[0, span] += dot(hid[j, span], wd[j], NN)
            part[1, span] += dot(gat[j, span], wg[j], NT) + dot(upg[j, span], wu[j], NT)
            return carry

        lax.fori_loop(1, local, body, 0)

    def ring(phase, way, arr, d):
        span = pl.ds(offsets[phase], sizes[phase])
        return pltpu.make_async_remote_copy(
            src_ref=red_out.at[way, arr, d - 1, span],
            dst_ref=red_in.at[way, arr, d - 1, span],
            send_sem=r_send.at[phase, way, arr, d - 1],
            recv_sem=r_recv.at[phase, way, arr, d - 1],
            device_id=(right, left)[way],
            device_id_type=MESH,
        )

    def forward(phase, way, arr, d):
        size, span = sizes[phase], pl.ds(offsets[phase], sizes[phase])
        value = part[arr, pl.ds(bases[phase] + slot(1 - way, d) * size, size)]
        if d < half - 1 or (d == half - 1 and arr == way):
            ring(phase, way, arr, d + 1).wait_recv()
            value = value + red_in[way, arr, d, span].astype(F32)
        red_out[way, arr, d - 1, span] = value.astype(BF16)
        move = ring(phase, way, arr, d)
        move.start()
        started.append(move)

    ticks = [(0, half)]
    for d in range(half - 1, 0, -1):
        ticks += [(1, d), (0, d)]
    waiting = [list(ticks), list(ticks)]

    def tick(phase, count=1):
        for arr, d in waiting[phase][:count]:
            forward(phase, 0, arr, d)
            forward(phase, 1, 1 - arr, d)
        waiting[phase] = waiting[phase][count:]

    def weight_grad(j, kind):
        buf = (gg_ref, gu_ref, gd_ref)[kind]
        if kind == 0:
            buf[j] = dot(xt[...], gat[j], NN).astype(BF16)
        elif kind == 1:
            buf[j] = dot(xt[...], upg[j], NN).astype(BF16)
        else:
            buf[j] = dot(hid[j], cs[:, pl.ds(0, width)], TN).astype(BF16)

    advance(0, 0)
    for t in range(1, half):
        advance(0, t)
        advance(1, t - 1)
    advance(0, half)
    for load in loads:
        load.wait()
    project(0)
    advance(1, half - 1)
    activate(0)
    combine(0)
    tick(0, 2)
    advance(1, half)
    project(1)
    tick(0)
    xt[...] = xs[...].T
    tick(0)
    activate(1)
    tick(0)
    combine(1)
    tick(1, 2)
    jobs = [(j, kind) for j in range(local) for kind in range(3)]
    while jobs or waiting[0] or waiting[1]:
        tick(0)
        left_ticks = max(1, len(waiting[1]))
        for job in jobs[:-(-len(jobs) // left_ticks)]:
            weight_grad(*job)
        jobs = jobs[-(-len(jobs) // left_ticks):]
        tick(1)

    for arr, ref in ((0, moe_ref), (1, gn_ref)):
        for phase in range(2):
            span = pl.ds(offsets[phase], sizes[phase])
            total = part[arr, pl.ds(bases[phase], sizes[phase])]
            for way in range(2):
                ring(phase, way, arr, 1).wait_recv()
                total = total + red_in[way, arr, 0, span].astype(F32)
            part[arr, span] = total
        ref[...] = part[arr, pl.ds(0, tokens)].astype(BF16)

    for move in started:
        move.wait_send()
    for chunk in range(2):
        for j in range(local):
            swap(chunk, j).wait_send()


def deliver(moe, grad, gg, gu, gd, moe_out, grad_out, gg_out, gu_out, gd_out, sem):
    copies = [
        pltpu.make_async_copy(src.at[j], dst.at[j], sem.at[i, j])
        for i, (src, dst) in enumerate(((gg, gg_out), (gu, gu_out), (gd, gd_out)))
        for j in range(src.shape[0])
    ]
    for copy in copies:
        copy.start()
    moe_out[...] = moe[...]
    grad_out[...] = grad[...]
    for copy in copies:
        copy.wait()


def fused(normed, cotangent, expert_ids, route_weights, w_gate, w_up, w_down):
    tok_rows, width = normed.shape
    local, _, hidden = w_gate.shape
    n = lax.axis_size("expert")
    experts = local * n
    rows = -(-tok_rows // 16) * 16
    tail = -(-2 * experts // 128) * 128
    total, half = n * rows, n // 2
    any_spec, vmem_spec = pl.BlockSpec(memory_space=pl.ANY), pl.BlockSpec(memory_space=pltpu.VMEM)
    dma = pltpu.SemaphoreType.DMA
    moe, grad, gg, gu, gd = pl.pallas_call(
        functools.partial(kernel, n, rows, width, experts),
        out_shape=(
            pltpu.VMEM((tok_rows, width), BF16),
            pltpu.VMEM((tok_rows, width), BF16),
            pltpu.VMEM(w_gate.shape, BF16),
            pltpu.VMEM(w_up.shape, BF16),
            pltpu.VMEM(w_down.shape, BF16),
        ),
        in_specs=[vmem_spec, vmem_spec, vmem_spec, vmem_spec, any_spec, any_spec, any_spec],
        out_specs=(vmem_spec, vmem_spec, vmem_spec, vmem_spec, vmem_spec),
        scratch_shapes=[
            pltpu.VMEM((total, width), BF16),
            pltpu.VMEM((total, width + tail), BF16),
            pltpu.VMEM((width, total), BF16),
            pltpu.VMEM(w_gate.shape, BF16),
            pltpu.VMEM(w_up.shape, BF16),
            pltpu.VMEM(w_down.shape, BF16),
            pltpu.VMEM((local, 3, total, hidden), F32),
            pltpu.VMEM((local, 3, total, hidden), BF16),
            pltpu.VMEM((local, 3, total, hidden), BF16),
            pltpu.VMEM((local, total, hidden), BF16),
            pltpu.VMEM((local, total, hidden), BF16),
            pltpu.VMEM((local, total, hidden), BF16),
            pltpu.VMEM((2, total, width), F32),
            pltpu.VMEM((2, 2, half, rows, width), BF16),
            pltpu.VMEM((2, 2, half, rows, width), BF16),
            dma((3,)),
            dma((2, 2, 2, half)),
            dma((2, 2, 2, half)),
            dma((2, local)),
            dma((2, local)),
            dma((2, 2, 2, half)),
            dma((2, 2, 2, half)),
        ],
        compiler_params=pltpu.CompilerParams(
            collective_id=0, has_side_effects=True, vmem_limit_bytes=46 * 2**20
        ),
    )(normed, cotangent, expert_ids.T, route_weights.T, w_gate, w_up, w_down)
    moe, grad, gg, gu, gd = (pltpu.with_memory_space_constraint(a, pltpu.VMEM) for a in (moe, grad, gg, gu, gd))
    shapes = tuple(jax.ShapeDtypeStruct(a.shape, BF16) for a in (moe, grad, gg, gu, gd))
    return pl.pallas_call(
        deliver,
        out_shape=shapes,
        in_specs=[vmem_spec] * 5,
        out_specs=(vmem_spec, vmem_spec, any_spec, any_spec, any_spec),
        scratch_shapes=[dma((3, local))],
        compiler_params=pltpu.CompilerParams(vmem_limit_bytes=4 * 2**20),
    )(moe, grad, gg, gu, gd)


def plain(normed, cotangent, routes, w_gate, w_up, w_down):
    local = w_gate.shape[0]
    rows = lax.all_gather(normed, "expert", axis=0, tiled=True)
    grads = lax.all_gather(cotangent, "expert", axis=0, tiled=True)
    probs = lax.all_gather(routes, "expert", axis=0, tiled=True)
    probs = lax.dynamic_slice_in_dim(probs, lax.axis_index("expert") * local, local, axis=1)
    p = probs.T[:, :, None]
    ein = functools.partial(jnp.einsum, preferred_element_type=F32)
    gate, up, back = lax.psum(
        (ein("rd,jdf->jrf", rows, w_gate), ein("rd,jdf->jrf", rows, w_up), ein("rd,jfd->jrf", grads, w_down)),
        "dp",
    )
    back = p * back
    sig = jax.nn.sigmoid(gate)
    act = gate * sig
    hid = (p * (act * up)).astype(BF16)
    gat = (back * up * sig * (1.0 + gate * (1.0 - sig))).astype(BF16)
    upg = (back * act).astype(BF16)
    moe = ein("jrf,jfd->rd", hid, w_down)
    grad = ein("jrf,jdf->rd", gat, w_gate) + ein("jrf,jdf->rd", upg, w_up)
    return (
        lax.psum_scatter(moe, "expert", scatter_dimension=0, tiled=True).astype(BF16),
        lax.psum_scatter(grad, "expert", scatter_dimension=0, tiled=True).astype(BF16),
        ein("rd,jrf->jdf", rows, gat).astype(BF16),
        ein("rd,jrf->jdf", rows, upg).astype(BF16),
        ein("jrf,rd->jfd", hid, grads).astype(BF16),
    )


def shards(normed, cotangent, expert_ids, route_weights, w_gate, w_up, w_down):
    n, pair = lax.axis_size("expert"), lax.axis_size("dp")
    experts = w_gate.shape[0] * n
    if pair == 2 and 4 <= n <= 8 and n % 4 == 0 and 16 < normed.shape[0] <= 128:
        return fused(normed, cotangent, expert_ids, route_weights, w_gate, w_up, w_down)
    chosen = expert_ids[:, :, None] == jnp.arange(experts, dtype=jnp.int32)[None, None, :]
    routes = jnp.sum(jnp.where(chosen, route_weights[:, :, None], 0.0), axis=1)
    return plain(normed, cotangent, routes, w_gate, w_up, w_down)


def solution(mesh):
    in_specs = (
        P(("groups", "expert"), "dp"),
        P(("groups", "expert"), "dp"),
        P(("groups", "expert"), None),
        P(("groups", "expert"), None),
        P("expert", "dp", None),
        P("expert", "dp", None),
        P("expert", None, "dp"),
    )
    out_specs = (
        P(("groups", "expert"), "dp"),
        P(("groups", "expert"), "dp"),
        P(("groups", "expert"), "dp", None),
        P(("groups", "expert"), "dp", None),
        P(("groups", "expert"), None, "dp"),
    )
    return jax.shard_map(shards, mesh=mesh, in_specs=in_specs, out_specs=out_specs, check_vma=False)
```

```python
import functools

import jax
import jax.numpy as jnp
from jax import lax
from jax.experimental import pallas as pl
from jax.experimental.pallas import tpu as pltpu
from jax.sharding import PartitionSpec as P

F32, BF16 = jnp.float32, jnp.bfloat16
NN = (((1,), (0,)), ((), ()))
NT = (((1,), (1,)), ((), ()))
TN = (((0,), (0,)), ((), ()))
MESH = pl.DeviceIdType.MESH


def dot(a, b, dims):
    return lax.dot_general(a, b, dims, preferred_element_type=F32)


def kernel(n, rows, width, experts, x_in, c_in, ids, weights, wg_hbm, wu_hbm, wd_hbm,
           moe_ref, gn_ref, gg_ref, gu_ref, gd_ref,
           xs, cs, xt, wg, wu, wd, own, snd, rcv, hid, gat, upg, part, red_out, red_in,
           w_sem, g_send, g_recv, d_send, d_recv, r_send, r_recv):
    half = n // 2
    local = wg.shape[0]
    me_g, me_e, me_d = lax.axis_index("groups"), lax.axis_index("expert"), lax.axis_index("dp")
    z, col = me_e // 2, me_e % 2
    pos = z + col * (n - 1 - 2 * z)

    def at(place):
        place = (place + n) % n
        upper = place // half
        return 2 * place + upper * (2 * n - 1 - 4 * place)

    right = (me_g, at(pos + 1), me_d)
    left = (me_g, at(pos - 1), me_d)
    mate = (me_g, me_e, 1 - me_d)

    loads = [
        pltpu.make_async_copy(src, dst, w_sem.at[i])
        for i, (src, dst) in enumerate(((wg_hbm, wg), (wu_hbm, wu), (wd_hbm, wd)))
    ]
    for load in loads:
        load.start()

    barrier = pltpu.get_barrier_semaphore()
    for other in (left, right, mate):
        pl.semaphore_signal(barrier, inc=1, device_id=other, device_id_type=MESH)
    tokens = x_in.shape[0]
    if rows > tokens:
        part[:, pl.ds(tokens, rows - tokens), :] = jnp.zeros((2, rows - tokens, width), F32)
    part[0, pl.ds(0, tokens), :] = x_in[...].astype(F32)
    part[1, pl.ds(0, tokens), :] = c_in[...].astype(F32)
    xs[pl.ds(0, rows), :] = part[0, pl.ds(0, rows), :].astype(BF16)
    cs[pl.ds(0, rows), pl.ds(0, width)] = part[1, pl.ds(0, rows), :].astype(BF16)
    tail = cs.shape[1] - width
    place = lax.broadcasted_iota(jnp.int32, (tail, tokens), 0)
    high, low = jnp.zeros((tail, tokens), F32), jnp.zeros((tail, tokens), F32)
    for k in range(ids.shape[0]):
        name, weight = ids[pl.ds(k, 1), :], weights[pl.ds(k, 1), :]
        high = high + jnp.where(place == name, weight, 0.0)
        low = low + jnp.where(place == name + experts, weight, 0.0)
    low = low - low.astype(BF16).astype(F32)
    part[0, pl.ds(0, tail), pl.ds(0, 128)] = jnp.zeros((tail, 128), F32)
    part[0, pl.ds(0, tail), pl.ds(0, tokens)] = high + low
    cs[pl.ds(0, rows), pl.ds(width, tail)] = part[0, pl.ds(0, tail), pl.ds(0, 128)].T[:rows].astype(BF16)
    pl.semaphore_wait(barrier, 3)

    def slot(way, t):
        if t == 0:
            return 0
        if t == half:
            return n - 1
        return 2 * t - 1 + way

    def gather(way, arr, t):
        buf = (xs, cs)[arr]
        return pltpu.make_async_remote_copy(
            src_ref=buf.at[pl.ds(slot(way, t - 1) * rows, rows)],
            dst_ref=buf.at[pl.ds(slot(way, t) * rows, rows)],
            send_sem=g_send.at[way, arr, t - 1],
            recv_sem=g_recv.at[way, arr, t - 1],
            device_id=(right, left)[way],
            device_id_type=MESH,
        )

    def moves(t):
        if t < half:
            return [gather(0, 0, t), gather(1, 0, t), gather(0, 1, t), gather(1, 1, t)]
        return [gather(0, 0, t), gather(1, 1, t)]

    started = []

    def advance(t):
        later = {0: moves(t + 1)} if t < half else {0: []}
        if t == 0:
            for move in later[0]:
                move.start()
        elif t < half - 1:
            for now, move in zip(moves(t), later[0]):
                now.wait_recv()
                move.start()
        elif t == half - 1:
            now = moves(t)
            now[0].wait_recv()
            later[0][0].start()
            now[3].wait_recv()
            later[0][1].start()
            now[1].wait_recv()
            now[2].wait_recv()
        else:
            for now in moves(t):
                now.wait_recv()
        started.extend(later[0])

    early = (n // 4) * 2 + 1
    spans = ((0, early * rows), (early * rows, (n - early) * rows))

    def swap(chunk, j):
        span = pl.ds(*spans[chunk])
        return pltpu.make_async_remote_copy(
            src_ref=snd.at[j, :, span],
            dst_ref=rcv.at[j, :, span],
            send_sem=d_send.at[chunk, j],
            recv_sem=d_recv.at[chunk, j],
            device_id=mate,
            device_id_type=MESH,
        )

    def project(chunk):
        span = pl.ds(*spans[chunk])

        def body(j):
            for m, value in enumerate((
                lambda: dot(xs[span, :], wg[j], NN),
                lambda: dot(xs[span, :], wu[j], NN),
                lambda: dot(cs[span, pl.ds(0, width)], wd[j], NT),
            )):
                result = value()
                own[j, m, span] = result
                snd[j, m, span] = result.astype(BF16)
            swap(chunk, j).start()

        for j in range(local):
            body(j)

    def activate(chunk):
        first, count = spans[chunk]
        span = pl.ds(first, count)

        def body(j):
            swap(chunk, j).wait_recv()
            tail = cs[span, pl.ds(width, cs.shape[1] - width)].astype(F32)
            lane = lax.broadcasted_iota(jnp.int32, tail.shape, 1)
            mine = me_e * local + j
            p = jnp.sum(
                jnp.where((lane == mine) | (lane == mine + experts), tail, 0.0), axis=1, keepdims=True
            )
            gate = own[j, 0, span] + rcv[j, 0, span].astype(F32)
            up = own[j, 1, span] + rcv[j, 1, span].astype(F32)
            back = p * (own[j, 2, span] + rcv[j, 2, span].astype(F32))
            sig = jax.nn.sigmoid(gate)
            act = gate * sig
            hid[j, span] = (p * (act * up)).astype(BF16)
            gat[j, span] = (back * up * sig * (1.0 + gate * (1.0 - sig))).astype(BF16)
            upg[j, span] = (back * act).astype(BF16)

        for j in range(local):
            body(j)

    def combine(chunk):
        span = pl.ds(*spans[chunk])
        part[0, span] = sum(dot(hid[j, span], wd[j], NN) for j in range(local))
        part[1, span] = sum(
            dot(gat[j, span], wg[j], NT) + dot(upg[j, span], wu[j], NT) for j in range(local)
        )

    for t in range(n // 4 + 1):
        advance(t)
    for load in loads:
        load.wait()
    project(0)
    for t in range(n // 4 + 1, half):
        advance(t)
    activate(0)
    combine(0)
    advance(half)
    project(1)
    xt[...] = xs[...].T
    activate(1)
    combine(1)

    def ring(way, arr, d):
        return pltpu.make_async_remote_copy(
            src_ref=red_out.at[way, arr, d - 1],
            dst_ref=red_in.at[way, arr, d - 1],
            send_sem=r_send.at[way, arr, d - 1],
            recv_sem=r_recv.at[way, arr, d - 1],
            device_id=(right, left)[way],
            device_id_type=MESH,
        )

    def forward(way, arr, d):
        value = part[arr, pl.ds(slot(1 - way, d) * rows, rows)]
        if d < half - 1 or (d == half - 1 and arr == way):
            ring(way, arr, d + 1).wait_recv()
            value = value + red_in[way, arr, d].astype(F32)
        red_out[way, arr, d - 1] = value.astype(BF16)
        move = ring(way, arr, d)
        move.start()
        started.append(move)

    def weight_grad(j, kind):
        buf = (gg_ref, gu_ref, gd_ref)[kind]
        if kind == 0:
            buf[j] = dot(xt[...], gat[j], NN).astype(BF16)
        elif kind == 1:
            buf[j] = dot(xt[...], upg[j], NN).astype(BF16)
        else:
            buf[j] = dot(hid[j], cs[:, pl.ds(0, width)], TN).astype(BF16)

    jobs = [(j, kind) for j in range(local) for kind in range(3)]
    ticks = [(0, half)]
    for d in range(half - 1, 0, -1):
        ticks += [(1, d), (0, d)]
    for i, (arr, d) in enumerate(ticks):
        forward(0, arr, d)
        forward(1, 1 - arr, d)
        if i >= 1:
            take = -(-len(jobs) // (len(ticks) - i))
            for job in jobs[:take]:
                weight_grad(*job)
            jobs = jobs[take:]

    for arr, ref in ((0, moe_ref), (1, gn_ref)):
        total = part[arr, pl.ds(0, rows)]
        for way in range(2):
            ring(way, arr, 1).wait_recv()
            total = total + red_in[way, arr, 0].astype(F32)
        part[arr, pl.ds(0, rows)] = total
        ref[...] = part[arr, pl.ds(0, tokens)].astype(BF16)

    for move in started:
        move.wait_send()
    for chunk in range(2):
        for j in range(local):
            swap(chunk, j).wait_send()


def deliver(moe, grad, gg, gu, gd, moe_out, grad_out, gg_out, gu_out, gd_out, sem):
    copies = [
        pltpu.make_async_copy(src.at[j], dst.at[j], sem.at[i, j])
        for i, (src, dst) in enumerate(((gg, gg_out), (gu, gu_out), (gd, gd_out)))
        for j in range(src.shape[0])
    ]
    for copy in copies:
        copy.start()
    moe_out[...] = moe[...]
    grad_out[...] = grad[...]
    for copy in copies:
        copy.wait()


def fused(normed, cotangent, expert_ids, route_weights, w_gate, w_up, w_down):
    tok_rows, width = normed.shape
    local, _, hidden = w_gate.shape
    n = lax.axis_size("expert")
    experts = local * n
    rows = -(-tok_rows // 16) * 16
    tail = -(-2 * experts // 128) * 128
    total, half = n * rows, n // 2
    any_spec, vmem_spec = pl.BlockSpec(memory_space=pl.ANY), pl.BlockSpec(memory_space=pltpu.VMEM)
    dma = pltpu.SemaphoreType.DMA
    moe, grad, gg, gu, gd = pl.pallas_call(
        functools.partial(kernel, n, rows, width, experts),
        out_shape=(
            pltpu.VMEM((tok_rows, width), BF16),
            pltpu.VMEM((tok_rows, width), BF16),
            pltpu.VMEM(w_gate.shape, BF16),
            pltpu.VMEM(w_up.shape, BF16),
            pltpu.VMEM(w_down.shape, BF16),
        ),
        in_specs=[vmem_spec, vmem_spec, vmem_spec, vmem_spec, any_spec, any_spec, any_spec],
        out_specs=(vmem_spec, vmem_spec, vmem_spec, vmem_spec, vmem_spec),
        scratch_shapes=[
            pltpu.VMEM((total, width), BF16),
            pltpu.VMEM((total, width + tail), BF16),
            pltpu.VMEM((width, total), BF16),
            pltpu.VMEM(w_gate.shape, BF16),
            pltpu.VMEM(w_up.shape, BF16),
            pltpu.VMEM(w_down.shape, BF16),
            pltpu.VMEM((local, 3, total, hidden), F32),
            pltpu.VMEM((local, 3, total, hidden), BF16),
            pltpu.VMEM((local, 3, total, hidden), BF16),
            pltpu.VMEM((local, total, hidden), BF16),
            pltpu.VMEM((local, total, hidden), BF16),
            pltpu.VMEM((local, total, hidden), BF16),
            pltpu.VMEM((2, total, width), F32),
            pltpu.VMEM((2, 2, half, rows, width), BF16),
            pltpu.VMEM((2, 2, half, rows, width), BF16),
            dma((3,)),
            dma((2, 2, half)),
            dma((2, 2, half)),
            dma((2, local)),
            dma((2, local)),
            dma((2, 2, half)),
            dma((2, 2, half)),
        ],
        compiler_params=pltpu.CompilerParams(
            collective_id=0, has_side_effects=True, vmem_limit_bytes=46 * 2**20
        ),
    )(normed, cotangent, expert_ids.T, route_weights.T, w_gate, w_up, w_down)
    moe, grad, gg, gu, gd = (pltpu.with_memory_space_constraint(a, pltpu.VMEM) for a in (moe, grad, gg, gu, gd))
    shapes = tuple(jax.ShapeDtypeStruct(a.shape, BF16) for a in (moe, grad, gg, gu, gd))
    return pl.pallas_call(
        deliver,
        out_shape=shapes,
        in_specs=[vmem_spec] * 5,
        out_specs=(vmem_spec, vmem_spec, any_spec, any_spec, any_spec),
        scratch_shapes=[dma((3, local))],
        compiler_params=pltpu.CompilerParams(vmem_limit_bytes=4 * 2**20),
    )(moe, grad, gg, gu, gd)


def plain(normed, cotangent, routes, w_gate, w_up, w_down):
    local = w_gate.shape[0]
    rows = lax.all_gather(normed, "expert", axis=0, tiled=True)
    grads = lax.all_gather(cotangent, "expert", axis=0, tiled=True)
    probs = lax.all_gather(routes, "expert", axis=0, tiled=True)
    probs = lax.dynamic_slice_in_dim(probs, lax.axis_index("expert") * local, local, axis=1)
    p = probs.T[:, :, None]
    ein = functools.partial(jnp.einsum, preferred_element_type=F32)
    gate, up, back = lax.psum(
        (ein("rd,jdf->jrf", rows, w_gate), ein("rd,jdf->jrf", rows, w_up), ein("rd,jfd->jrf", grads, w_down)),
        "dp",
    )
    back = p * back
    sig = jax.nn.sigmoid(gate)
    act = gate * sig
    hid = (p * (act * up)).astype(BF16)
    gat = (back * up * sig * (1.0 + gate * (1.0 - sig))).astype(BF16)
    upg = (back * act).astype(BF16)
    moe = ein("jrf,jfd->rd", hid, w_down)
    grad = ein("jrf,jdf->rd", gat, w_gate) + ein("jrf,jdf->rd", upg, w_up)
    return (
        lax.psum_scatter(moe, "expert", scatter_dimension=0, tiled=True).astype(BF16),
        lax.psum_scatter(grad, "expert", scatter_dimension=0, tiled=True).astype(BF16),
        ein("rd,jrf->jdf", rows, gat).astype(BF16),
        ein("rd,jrf->jdf", rows, upg).astype(BF16),
        ein("jrf,rd->jfd", hid, grads).astype(BF16),
    )


def shards(normed, cotangent, expert_ids, route_weights, w_gate, w_up, w_down):
    n, pair = lax.axis_size("expert"), lax.axis_size("dp")
    experts = w_gate.shape[0] * n
    if pair == 2 and 4 <= n <= 8 and n % 4 == 0:
        return fused(normed, cotangent, expert_ids, route_weights, w_gate, w_up, w_down)
    chosen = expert_ids[:, :, None] == jnp.arange(experts, dtype=jnp.int32)[None, None, :]
    routes = jnp.sum(jnp.where(chosen, route_weights[:, :, None], 0.0), axis=1)
    return plain(normed, cotangent, routes, w_gate, w_up, w_down)


def solution(mesh):
    in_specs = (
        P(("groups", "expert"), "dp"),
        P(("groups", "expert"), "dp"),
        P(("groups", "expert"), None),
        P(("groups", "expert"), None),
        P("expert", "dp", None),
        P("expert", "dp", None),
        P("expert", None, "dp"),
    )
    out_specs = (
        P(("groups", "expert"), "dp"),
        P(("groups", "expert"), "dp"),
        P(("groups", "expert"), "dp", None),
        P(("groups", "expert"), "dp", None),
        P(("groups", "expert"), None, "dp"),
    )
    return jax.shard_map(shards, mesh=mesh, in_specs=in_specs, out_specs=out_specs, check_vma=False)
```
